32 devices in a mesh: wide: 32 (over z, y, x, core).
Axes of the slice: x: 2, y: 2, z: 4, core: 2. Of those that a mesh axis runs over, the one named last changes fastest.
Arguments:
- features: bfloat16 [49152, 2048], P('wide'), may hold values from -6 to 6
- group_ids: int32 [32], P('wide'), may hold values from 0 to 3, as said below
- reducer: bfloat16 [2048, 512], replicated, may hold values from -0.125 to 0.125
- spatial: bfloat16 [4608, 512], replicated, may hold values from -0.09375 to 0.09375
- expander: bfloat16 [512, 2048], replicated, may hold values from -0.25 to 0.25
- gain_first: float32 [512], replicated, may hold values from 0.5 to 1.5
- bias_first: float32 [512], replicated, may hold values from -3 to 3
- gain_middle: float32 [512], replicated, may hold values from 0.5 to 1.5
- bias_middle: float32 [512], replicated, may hold values from -3 to 3
- gain_last: float32 [2048], replicated, may hold values from 0.5 to 1.5
- bias_last: float32 [2048], replicated, may hold values from -3 to 3
- upstream: bfloat16 [49152, 2048], P('wide'), may hold values from -6 to 6
Outputs:
- block_out: bfloat16 [49152, 2048], P('wide')
- features_grad: bfloat16 [49152, 2048], P('wide')
- reducer_grad: float32 [2048, 512], replicated
- spatial_grad: float32 [4608, 512], replicated
- expander_grad: float32 [512, 2048], replicated
- gain_first_gradient: float32 [512], replicated
- bias_first_gradient: float32 [512], replicated
- gain_middle_gradient: float32 [512], replicated
- bias_middle_gradient: float32 [512], replicated
- gain_last_gradient: float32 [2048], replicated
- bias_last_gradient: float32 [2048], replicated
The draws below stay inside these ranges and needn't reach their ends.
Inputs may be any that keep to these rules, and one draw needn't show every extreme that they name: `group_ids`: each of the four ids is held by exactly 8 devices.
All inputs are finite; a program needn't handle non-finite values.
Results may differ from the reference program's by a relative error of at most 0.0085.
Values sent between devices are 32-bit elements; how exact they have to be, the bound alone decides.
No kernel may reach another device: no remote copies, remote signals or barrier semaphores. Data moves between devices by JAX's collectives and lax.ppermute only.
A program may use at most 192 MiB of HBM per device.

```python
import jax
import jax.numpy as jnp
from jax import lax

C = 2048
M = 512
PIXELS = 49152
N_WIDE = 32


def draw_group_ids(key, part):
    key = jax.random.fold_in(key, 11)
    return (jax.random.permutation(key, N_WIDE) % 4).astype(jnp.int32)


def steps_of(own_key, dims, pieces, least, high):
    def one(axis_at, parts):
        heights = jax.random.uniform(jax.random.fold_in(jax.random.fold_in(own_key, 6), axis_at), (parts,), jnp.float32, least / len(pieces), high / len(pieces))
        return jnp.repeat(jnp.exp(heights), dims[axis_at] // parts).reshape((-1,) + (1,) * (len(dims) - axis_at - 1))

    factor_of = one(*pieces[0])
    for cut in pieces[1:]:
        factor_of = factor_of * one(*cut)
    return factor_of


def normal_values(own_key, extent, scale, bound, shards=(), held_as=jnp.bfloat16):
    loudness = steps_of(own_key, extent, shards, -0.22, 0.18) if shards else 1.0
    values = jax.random.normal(own_key, extent, jnp.float32) * scale * loudness
    return jnp.minimum(jnp.maximum(values, -bound), bound).astype(held_as)


def setup_inputs(seed: int = 0) -> dict:
    key_list = jax.random.split(jax.random.key(seed), 13)
    features = normal_values(key_list[0], (PIXELS, C), 1.0, 6.0, ((0, 32),))
    group_ids = draw_group_ids(jax.random.fold_in(key_list[12], 71), 0)
    reducer = normal_values(key_list[2], (C, M), C ** -0.5, 0.125)
    spatial = normal_values(key_list[3], (9 * M, M), (9 * M) ** -0.5, 0.09375)
    expander = normal_values(key_list[4], (M, C), M ** -0.5, 0.25)
    gain_first = jnp.clip(1.0 + 0.1 * jax.random.normal(key_list[5], (M,), jnp.float32), 0.5, 1.5)
    bias_first = normal_values(key_list[6], (M,), 0.5, 3.0, (), jnp.float32)
    gain_middle = jnp.clip(1.0 + 0.1 * jax.random.normal(key_list[7], (M,), jnp.float32), 0.5, 1.5)
    bias_middle = normal_values(key_list[8], (M,), 0.5, 3.0, (), jnp.float32)
    gain_last = jnp.clip(1.0 + 0.1 * jax.random.normal(key_list[9], (C,), jnp.float32), 0.5, 1.5)
    bias_last = normal_values(key_list[10], (C,), 0.5, 3.0, (), jnp.float32)
    upstream = normal_values(key_list[11], (PIXELS, C), 1.0, 6.0, ((0, 32),))
    return {"features": features, "group_ids": group_ids, "reducer": reducer, "spatial": spatial, "expander": expander, "gain_first": gain_first, "bias_first": bias_first, "gain_middle": gain_middle, "bias_middle": bias_middle, "gain_last": gain_last, "bias_last": bias_last, "upstream": upstream}


epsilon = 1e-05

@jax.custom_vjp
def low(v):
    return lax.optimization_barrier(v.astype(jnp.bfloat16)).astype(jnp.float32)

@jax.custom_vjp
def low_back(v):
    return v

def low_keep(v):
    return (low(v), None)

def low_pass(kept, grad):
    return (grad,)

def back_keep(v):
    return (v, None)

def back_low(kept, grad):
    return (low(grad),)
low.defvjp(low_keep, low_pass)
low_back.defvjp(back_keep, back_low)

def reference(features, group_ids, reducer, spatial, expander, gain_first, bias_first, gain_middle, bias_middle, gain_last, bias_last, upstream):
    devices = group_ids.shape[0]
    rows = features.shape[0] // devices
    width = spatial.shape[1]
    highest = lax.Precision.HIGHEST
    side = jnp.where(group_ids == 3, 2, 5 + group_ids).astype(jnp.int32)
    area = side * side
    positions = jnp.arange(rows, dtype=jnp.int32)[None, :]
    images = positions // area[:, None]
    within = positions % area[:, None]
    row_pos = within // side[:, None]
    col_pos = within % side[:, None]
    valid = (images < (rows // area)[:, None]).astype(jnp.float32)
    picker = jnp.stack([group_ids != 3, group_ids == 3], axis=1).astype(jnp.float32)
    shifts = []
    windows = []
    for delta_row in (-1, 0, 1):
        for delta_col in (-1, 0, 1):
            shifts.append((delta_row * side + delta_col).astype(jnp.int32))
            inside = (row_pos + delta_row >= 0) & (row_pos + delta_row < side[:, None]) & (col_pos + delta_col >= 0) & (col_pos + delta_col < side[:, None])
            windows.append(inside.astype(jnp.float32))

    def roll_rows(block, amounts):
        return jax.vmap(lambda values, amount: jnp.roll(values, amount, axis=0))(block, amounts)

    def product(left, right):
        return jnp.einsum('npc,cm->npm', left, right, precision=highest)

    def normalize(values, gain, bias):
        counts = lax.optimization_barrier(jnp.sum(valid, axis=1))
        number = jnp.einsum('nk,n->k', picker, counts, precision=highest)
        totals = jnp.einsum('nk,nc->kc', picker, lax.optimization_barrier(jnp.sum(valid[..., None] * values, axis=1)), precision=highest)
        mean = jnp.einsum('nk,kc->nc', picker, totals / number[:, None], precision=highest)
        centered = values - mean[:, None, :]
        spread = jnp.einsum('nk,nc->kc', picker, lax.optimization_barrier(jnp.sum(valid[..., None] * centered * centered, axis=1)), precision=highest) / number[:, None]
        inverse = jnp.einsum('nk,kc->nc', picker, lax.rsqrt(spread + epsilon), precision=highest)
        return centered * inverse[:, None, :] * gain + bias

    def forward(inputs_full, reducer_full, spatial_full, expander_full, gain_one, bias_one, gain_two, bias_two, gain_three, bias_three):
        pre_first = low_back(product(inputs_full, reducer_full))
        act_first = normalize(pre_first, gain_one, bias_one)
        low_first = low(jax.nn.silu(act_first) * valid[..., None])
        pre_middle = jnp.zeros(low_first.shape, jnp.float32)
        for tap_index in range(9):
            shifted = roll_rows(low_first, -shifts[tap_index]) * windows[tap_index][..., None]
            pre_middle = pre_middle + product(shifted, spatial_full[tap_index * width:(tap_index + 1) * width])
        pre_middle = low_back(pre_middle)
        act_middle = normalize(pre_middle, gain_two, bias_two)
        low_middle = low(jax.nn.silu(act_middle) * valid[..., None])
        pre_last = low_back(product(low_middle, expander_full))
        act_last = normalize(pre_last, gain_three, bias_three)
        return jax.nn.silu(act_last + inputs_full) * valid[..., None]
    primals = (features.astype(jnp.float32).reshape(devices, rows, -1), reducer.astype(jnp.float32), spatial.astype(jnp.float32), expander.astype(jnp.float32), gain_first, bias_first, gain_middle, bias_middle, gain_last, bias_last)
    outputs, pullback = jax.vjp(forward, *primals)
    grads = pullback(upstream.astype(jnp.float32).reshape(devices, rows, -1))
    return (outputs.reshape(features.shape).astype(jnp.bfloat16), grads[0].reshape(features.shape).astype(jnp.bfloat16), grads[1], grads[2], grads[3], grads[4], grads[5], grads[6], grads[7], grads[8], grads[9])
```

```python
import jax
import jax.numpy as jnp
from jax import lax
from jax.sharding import PartitionSpec as P

epsilon = 1e-05


def silu_slope(values):
    sigma = jax.nn.sigmoid(values)
    return sigma * (1.0 + values * (1.0 - sigma))


def contract_rows(left, right):
    return lax.dot_general(
        left, right, (((0,), (0,)), ((), ())), preferred_element_type=jnp.float32
    )


def contract_cols(left, right):
    return lax.dot_general(
        left, right, (((1,), (1,)), ((), ())), preferred_element_type=jnp.float32
    )


def layout(group_value, rows):
    side = jnp.where(group_value == 3, 2, 5 + group_value)
    area = side * side
    positions = jnp.arange(rows, dtype=jnp.int32)
    images = positions // area
    within = positions % area
    row_pos = within // side
    col_pos = within % side
    valid = (images < rows // area).astype(jnp.float32)
    shifts = []
    windows = []
    for delta_row in (-1, 0, 1):
        for delta_col in (-1, 0, 1):
            shifts.append(delta_row * side + delta_col)
            inside = (
                (row_pos + delta_row >= 0)
                & (row_pos + delta_row < side)
                & (col_pos + delta_col >= 0)
                & (col_pos + delta_col < side)
            )
            windows.append(inside.astype(jnp.float32))
    return (valid, shifts, windows)


def own_row(picker, table):
    return jnp.sum(picker[:, None] * table, axis=0)


class Wide:
    def __init__(self, devices):
        self.devices = devices
        self.bits = [1 << k for k in range(devices.bit_length() - 1)]

    def swap(self, value, bit):
        pairs = [(i, i ^ bit) for i in range(self.devices)]
        return lax.ppermute(value, "wide", pairs)

    def high(self, bit):
        return (lax.axis_index("wide") & bit) != 0

    def total(self, value):
        for bit in self.bits:
            value = value + self.swap(value, bit)
        return value

    def merge_counts(self, counts):
        stages = []
        for bit in self.bits:
            other = self.swap(counts, bit)
            stages.append((counts, other))
            counts = counts + other
        return stages, counts

    def merge_moments(self, mean, square, stages):
        for bit, (own, other) in zip(self.bits, stages):
            packed = self.swap(jnp.concatenate([mean, square], axis=0), bit)
            gap = packed[:2] - mean
            share = other / jnp.maximum(own + other, 1.0)
            mean = mean + gap * share[:, None]
            square = square + packed[2:] + gap * gap * (own * share)[:, None]
        return mean, square

    def sum_replicated(self, value):
        for bit in self.bits:
            half = value.shape[0] // 2
            place = self.high(bit).astype(jnp.int32)
            sent = lax.dynamic_slice_in_dim(value, (1 - place) * half, half)
            kept = lax.dynamic_slice_in_dim(value, place * half, half)
            value = kept + self.swap(sent, bit)
        for bit in self.bits[::-1]:
            other = self.swap(value, bit)
            up = self.high(bit)
            value = jnp.concatenate(
                [jnp.where(up, other, value), jnp.where(up, value, other)], axis=0
            )
        return value


def stream_stats(values, valid, picker, wide, stages, number):
    own_count = jnp.sum(valid)
    weights = valid[:, None]
    mean = jnp.sum(weights * values, axis=0) / own_count
    centered = values - mean
    square = jnp.sum(weights * centered * centered, axis=0)
    means, squares = wide.merge_moments(
        picker[:, None] * mean[None, :], picker[:, None] * square[None, :], stages
    )
    variance = own_row(picker, squares) / number
    return (own_row(picker, means), lax.rsqrt(variance + epsilon))


def norm_back(grad_norm, normed, gain, inverse, number, valid, picker, wide):
    first = jnp.sum(grad_norm, axis=0)
    second = jnp.sum(grad_norm * normed, axis=0)
    sums = wide.total(
        jnp.concatenate([picker[:, None] * first[None, :], picker[:, None] * second[None, :]])
    )
    totals, products = sums[:2], sums[2:]
    own_total = own_row(picker, totals)
    own_product = own_row(picker, products)
    grad_in = (
        valid[:, None]
        * (gain * inverse)
        * (grad_norm - (own_total + normed * own_product) / number)
    )
    return (grad_in, jnp.sum(products, axis=0), jnp.sum(totals, axis=0))


def on_device(
    wide,
    features,
    group_ids,
    reducer,
    spatial,
    expander,
    gain_first,
    bias_first,
    gain_middle,
    bias_middle,
    gain_last,
    bias_last,
    upstream,
):
    rows = features.shape[0]
    width = spatial.shape[1]
    group_value = group_ids[0]
    picker = jnp.stack([group_value != 3, group_value == 3]).astype(jnp.float32)
    valid, shifts, windows = layout(group_value, rows)
    valid_col = valid[:, None]
    stages, counts = wide.merge_counts(picker * jnp.sum(valid))
    number = jnp.sum(picker * counts)
    pre_first = jnp.dot(features, reducer, preferred_element_type=jnp.float32)
    mean_first, inverse_first = stream_stats(pre_first, valid, picker, wide, stages, number)
    normed_first = (pre_first - mean_first) * inverse_first
    act_first = normed_first * gain_first + bias_first
    low_first = (jax.nn.silu(act_first) * valid_col).astype(jnp.bfloat16)
    columns = jnp.concatenate(
        [
            jnp.roll(low_first, -shifts[tap_index], axis=0)
            * windows[tap_index][:, None].astype(jnp.bfloat16)
            for tap_index in range(9)
        ],
        axis=1,
    )
    pre_middle = jnp.dot(columns, spatial, preferred_element_type=jnp.float32)
    mean_middle, inverse_middle = stream_stats(pre_middle, valid, picker, wide, stages, number)
    normed_middle = (pre_middle - mean_middle) * inverse_middle
    act_middle = normed_middle * gain_middle + bias_middle
    low_middle = (jax.nn.silu(act_middle) * valid_col).astype(jnp.bfloat16)
    pre_last = jnp.dot(low_middle, expander, preferred_element_type=jnp.float32)
    mean_last, inverse_last = stream_stats(pre_last, valid, picker, wide, stages, number)
    normed_last = (pre_last - mean_last) * inverse_last
    act_last = normed_last * gain_last + bias_last
    summed = act_last + features.astype(jnp.float32)
    block_out = (jax.nn.silu(summed) * valid_col).astype(jnp.bfloat16)
    grad_summed = upstream.astype(jnp.float32) * valid_col * silu_slope(summed)
    grad_pre_last, gain_last_gradient, bias_last_gradient = norm_back(
        grad_summed, normed_last, gain_last, inverse_last, number, valid, picker, wide
    )
    low_grad_last = grad_pre_last.astype(jnp.bfloat16)
    expander_grad = lax.psum(contract_rows(low_middle, low_grad_last), "wide")
    grad_low_middle = contract_cols(low_grad_last, expander)
    grad_act_middle = grad_low_middle * valid_col * silu_slope(act_middle)
    grad_pre_middle, gain_middle_gradient, bias_middle_gradient = norm_back(
        grad_act_middle, normed_middle, gain_middle, inverse_middle, number, valid, picker, wide
    )
    low_grad_middle = grad_pre_middle.astype(jnp.bfloat16)
    spatial_grad = wide.sum_replicated(contract_rows(columns, low_grad_middle))
    grad_columns = contract_cols(low_grad_middle, spatial)
    grad_low_first = jnp.zeros((rows, width), jnp.float32)
    for tap_index in range(9):
        block = (
            grad_columns[:, tap_index * width : (tap_index + 1) * width]
            * windows[tap_index][:, None]
        )
        grad_low_first = grad_low_first + jnp.roll(block, shifts[tap_index], axis=0)
    grad_act_first = grad_low_first * valid_col * silu_slope(act_first)
    grad_pre_first, gain_first_gradient, bias_first_gradient = norm_back(
        grad_act_first, normed_first, gain_first, inverse_first, number, valid, picker, wide
    )
    low_grad_first = grad_pre_first.astype(jnp.bfloat16)
    reducer_grad = wide.sum_replicated(contract_rows(features, low_grad_first))
    features_grad = (contract_cols(low_grad_first, reducer) + grad_summed).astype(jnp.bfloat16)
    return (
        block_out,
        features_grad,
        reducer_grad,
        spatial_grad,
        expander_grad,
        gain_first_gradient,
        bias_first_gradient,
        gain_middle_gradient,
        bias_middle_gradient,
        gain_last_gradient,
        bias_last_gradient,
    )


def solution(mesh):
    wide = Wide(mesh.shape["wide"])
    in_specs = (
        P("wide", None),
        P("wide"),
        P(),
        P(),
        P(),
        P(),
        P(),
        P(),
        P(),
        P(),
        P(),
        P("wide", None),
    )
    out_specs = (P("wide", None), P("wide", None), P(), P(), P(), P(), P(), P(), P(), P(), P())

    def body(*arrays):
        return on_device(wide, *arrays)

    return jax.shard_map(body, mesh=mesh, in_specs=in_specs, out_specs=out_specs, check_vma=False)
```

```python
import functools

import jax
import jax.numpy as jnp
from jax import lax
from jax.experimental import pallas as pl
from jax.experimental.pallas import tpu as pltpu
from jax.sharding import PartitionSpec as P

epsilon = 1e-05
pad = 8
lane = 256
shared = 2
ragged = 64
VM = pl.BlockSpec(memory_space=pltpu.VMEM)
SM = pl.BlockSpec(memory_space=pltpu.SMEM)
ANY = pl.BlockSpec(memory_space=pl.ANY)
HBM = pl.BlockSpec(memory_space=pltpu.HBM)
OFFSETS = [(r, c) for r in (-1, 0, 1) for c in (-1, 0, 1)]


def params(mib):
    return pltpu.CompilerParams(vmem_limit_bytes=mib * 1024 * 1024)


def cost(flops, moved):
    return pl.CostEstimate(flops=int(flops), bytes_accessed=int(moved), transcendentals=0)


def struct(shape, dtype=jnp.float32):
    return jax.ShapeDtypeStruct(shape, dtype)


def dot(left, right):
    return jnp.dot(left, right, preferred_element_type=jnp.float32)


def dot_cols(left, right):
    return lax.dot_general(
        left, right, (((1,), (1,)), ((), ())), preferred_element_type=jnp.float32
    )


def dot_rows(left, right):
    return lax.dot_general(
        left, right, (((0,), (0,)), ((), ())), preferred_element_type=jnp.float32
    )


def sigmoid(v):
    return 0.5 * jnp.tanh(0.5 * v) + 0.5


def slope_of(act):
    sig = sigmoid(act)
    value = act * sig
    return sig + value * (1.0 - sig)


def row_ids(start, rows, width):
    return lax.broadcasted_iota(jnp.int32, (rows, width), 0) + start


def fill(values, filled, start=0, total=None):
    rows, width = values.shape
    total = rows if total is None else total
    safe = max(0, min(rows, total - ragged - start))
    if safe == rows:
        return values
    rest = jnp.where(row_ids(start + safe, rows - safe, width) < filled, values[safe:], 0.0)
    return rest if safe == 0 else jnp.concatenate([values[:safe], rest], axis=0)


def column_sum(values):
    return jnp.sum(values, axis=0, keepdims=True)


def moments(values, filled, count):
    mean = column_sum(fill(values, filled)) / count
    gap = fill(values - mean, filled)
    return mean, column_sum(gap * gap)


def put_rows(packed, stream, at, row):
    packed[at : at + 1, :] = jnp.where(stream == 0, row, 0.0)
    packed[at + 1 : at + 2, :] = jnp.where(stream == 0, 0.0, row)


def pick(table, stream, at):
    return jnp.where(stream == 0, table[at : at + 1, :], table[at + 1 : at + 2, :])


def pair_up(tables, join):
    tables = list(tables)
    while len(tables) > 1:
        tables = [join(tables[k], tables[k + 1]) for k in range(0, len(tables), 2)]
    return tables[0]


def join_moments(left, right):
    mean, square, count = left
    other_mean, other_square, other_count = right
    number = count + other_count
    share = other_count / jnp.maximum(number, 1.0)
    gap = other_mean - mean
    return (
        mean + gap * share,
        square + other_square + gap * gap * (count * share),
        number,
    )


def merge_norm(tables, tallies, stream):
    mean, square, number = pair_up(
        [
            (pick(table, stream, 0), pick(table, stream, 2), pick(tally, stream, 4))
            for table, tally in zip(tables, tallies)
        ],
        join_moments,
    )
    return mean, lax.rsqrt(square / number + epsilon), number


def sum_tables(tables, stream, at):
    return pair_up([pick(table, stream, at) for table in tables], lambda a, b: a + b)


def first_kernel(ints, features, reducer, pre, packed, held, weights, sems):
    rows, depth = features.shape
    pieces = held.shape[0] // (held.shape[0] // (sems.shape[0] - 1))
    tile = rows // pieces
    load = pltpu.make_async_copy(reducer, weights, sems.at[pieces])
    load.start()
    copies = []
    for k in range(pieces):
        at = pl.ds(k * tile, tile)
        copies.append(pltpu.make_async_copy(features.at[at, :], held.at[at, :], sems.at[k]))
    for copy in copies:
        copy.start()
    load.wait()
    filled, stream = ints[1], ints[2]
    parts = []

    def settle(k):
        values = pre[k * tile : (k + 1) * tile, :]
        count = jnp.minimum(filled - k * tile, tile).astype(jnp.float32)
        mean = column_sum(fill(values, filled, k * tile, rows)) / count
        gap = fill(values - mean, filled, k * tile, rows)
        parts.append((mean, column_sum(gap * gap), jnp.full_like(mean, count)))

    for k in range(pieces):
        copies[k].wait()
        at = slice(k * tile, (k + 1) * tile)
        pre[at, :] = dot(held[at, :], weights[...])
        if k:
            settle(k - 1)
    settle(pieces - 1)
    mean, square, count = functools.reduce(join_moments, parts)
    put_rows(packed, stream, 0, mean)
    put_rows(packed, stream, 2, square)
    put_rows(packed, stream, 4, count)
    packed[6:8, :] = jnp.zeros((2, mean.shape[1]), jnp.float32)


def first_stage(ints, features, reducer, pieces=3):
    rows, depth = features.shape
    width = reducer.shape[1]
    return pl.pallas_call(
        first_kernel,
        in_specs=[SM, ANY, ANY],
        out_specs=[VM, VM],
        out_shape=[struct((rows, width)), struct((8, width))],
        scratch_shapes=[
            pltpu.VMEM((rows, depth), jnp.bfloat16),
            pltpu.VMEM((depth, width), jnp.bfloat16),
            pltpu.SemaphoreType.DMA((pieces + 1,)),
        ],
        compiler_params=params(50),
        cost_estimate=cost(2 * rows * depth * width, 12e6),
        name="first_stage",
    )(ints, features, reducer)


def place(start, rows, side):
    rows_f = (row_ids(start, rows, 128)).astype(jnp.float32) + 0.5
    side_f = side.astype(jnp.float32)
    area_f = side_f * side_f
    within = rows_f - jnp.floor(rows_f / area_f) * area_f
    high = jnp.floor(within / side_f)
    across = jnp.floor(within - high * side_f)
    return high, across


def inside(high, across, side, delta_row, delta_col):
    last = side.astype(jnp.float32) - 1.0
    parts = []
    if delta_row < 0:
        parts.append(high > 0.0)
    if delta_row > 0:
        parts.append(high < last)
    if delta_col < 0:
        parts.append(across > 0.0)
    if delta_col > 0:
        parts.append(across < last)
    keep = parts[0]
    for part in parts[1:]:
        keep = keep & part
    return keep


def spread(mask, width):
    return jnp.concatenate([mask] * (width // 128), axis=1)


def moved(held, start, rows):
    width = held.shape[1]
    base = pl.multiple_of((start // 8) * 8, 8)
    extra = start - base
    tiles = held[pl.ds(base, rows + 8), :].reshape(rows // 8 + 1, 8, width)
    tiles = pltpu.roll(tiles, lax.rem(8 - extra, 8), axis=1)
    first = lax.broadcasted_iota(jnp.int32, (1, 8, width), 1) < 8 - extra
    return jnp.where(first, tiles[:-1], tiles[1:]).reshape(rows, width)


def hold(held, values, rows):
    held[0:pad, :] = jnp.zeros((pad, held.shape[1]), jnp.float32)
    held[pad + rows :, :] = jnp.zeros((2 * pad, held.shape[1]), jnp.float32)
    held[pad : pad + rows, :] = values.astype(jnp.bfloat16).astype(jnp.float32)


def keep_norm(norm, mean, inverse, gain, bias, number):
    norm[0:1, :] = mean
    norm[1:2, :] = inverse
    norm[2:3, :] = gain
    norm[3:4, :] = bias
    norm[4:5, :] = number
    norm[5:8, :] = jnp.zeros((3, mean.shape[1]), jnp.float32)


def stream_weights(spatial, weights, sems):
    rows = spatial.shape[0] // 3
    copies = []
    for k in range(3):
        at = pl.ds(k * rows, rows)
        copies.append(pltpu.make_async_copy(spatial.at[at, :], weights.at[at, :], sems.at[k]))
        copies[k].start()
    return copies


def middle_kernel(ints, *refs):
    tables, refs = refs[:-11], refs[-11:]
    gain, bias, pre, spatial, low, out, packed, norm, held, weights, sems = refs
    side, filled, stream = ints[0], ints[1], ints[2]
    rows, width = pre.shape
    copies = stream_weights(spatial, weights, sems)
    mean, inverse, number = merge_norm(tables, tables, stream)
    keep_norm(norm, mean, inverse, gain[...], bias[...], number)
    act = (pre[...] - mean) * (inverse * gain[...]) + bias[...]
    value = fill(act * sigmoid(act), filled)
    low[...] = value.astype(jnp.bfloat16)
    hold(held, value, rows)
    high, across = place(0, rows, side)
    total = jnp.zeros((rows, width), jnp.float32)
    for tap, (dr, dc) in enumerate(OFFSETS):
        piece = moved(held, pad + dr * side + dc, rows)
        if (dr, dc) != (0, 0):
            piece = jnp.where(spread(inside(high, across, side, dr, dc), width), piece, 0.0)
        if tap % 3 == 0:
            copies[tap // 3].wait()
        total += dot(piece.astype(jnp.bfloat16), weights[tap * width : (tap + 1) * width, :])
    out[...] = total
    mean, square = moments(out[...], filled, filled.astype(jnp.float32))
    put_rows(packed, stream, 0, mean)
    put_rows(packed, stream, 2, square)


def middle_stage(ints, tables, gain, bias, pre, spatial):
    rows, width = pre.shape
    return pl.pallas_call(
        middle_kernel,
        in_specs=[SM] + [VM] * (len(tables) + 3) + [HBM],
        out_specs=[VM, VM, VM, VM],
        out_shape=[
            struct((rows, width), jnp.bfloat16),
            struct((rows, width)),
            struct((4, width)),
            struct((8, width)),
        ],
        scratch_shapes=[
            pltpu.VMEM((rows + 3 * pad, width), jnp.float32),
            pltpu.VMEM(spatial.shape, jnp.bfloat16),
            pltpu.SemaphoreType.DMA((3,)),
        ],
        compiler_params=params(40),
        cost_estimate=cost(18 * rows * width * width, 12e6),
        name="middle_stage",
    )(ints, *tables, gain, bias, pre, spatial)


def last_kernel(ints, *refs):
    tables, refs = refs[:-7], refs[-7:]
    tables, tallies = tables[: len(tables) // 2], tables[len(tables) // 2 :]
    gain, bias, pre, expander, low, packed, norm = refs
    filled, stream = ints[1], ints[2]
    rows, width = pre.shape
    wide = expander.shape[1]
    mean, inverse, number = merge_norm(tables, tallies, stream)
    keep_norm(norm, mean, inverse, gain[...], bias[...], number)
    act = (pre[...] - mean) * (inverse * gain[...]) + bias[...]
    low[...] = fill(act * sigmoid(act), filled).astype(jnp.bfloat16)
    count = filled.astype(jnp.float32)
    for k in range(wide // width):
        at = slice(k * width, (k + 1) * width)
        mean, square = moments(dot(low[...], expander[:, at]), filled, count)
        put_rows(packed.at[:, at], stream, 0, mean)
        put_rows(packed.at[:, at], stream, 2, square)


def last_stage(ints, tables, tallies, gain, bias, pre, expander):
    rows, width = pre.shape
    wide = expander.shape[1]
    return pl.pallas_call(
        last_kernel,
        in_specs=[SM] + [VM] * (2 * len(tables) + 4),
        out_specs=[VM, VM, VM],
        out_shape=[
            struct((rows, width), jnp.bfloat16),
            struct((4, wide)),
            struct((8, width)),
        ],
        compiler_params=params(34),
        cost_estimate=cost(2 * rows * width * wide, 8e6),
        name="last_stage",
    )(ints, *tables, *tallies, gain, bias, pre, expander)


def head_kernel(ints, *refs):
    tables, refs = refs[:-13], refs[-13:]
    tables, tallies = tables[: len(tables) // 2], tables[len(tables) // 2 :]
    gain, bias, low, expander, features, upstream = refs[:6]
    out, grad, part, packed, norm, hat, raw = refs[6:]
    filled, stream = ints[1], ints[2]
    rows, width = low.shape
    tile = expander.shape[1]
    chunk = 384
    count = filled.astype(jnp.float32)
    mean, inverse, number = merge_norm(tables, tallies, stream)
    keep_norm(norm, mean, inverse, gain[...], bias[...], number)
    hat[...] = dot(low[...], expander[...])
    scale = 0.5 * gain[...] * inverse
    offset = 0.5 * bias[...] - mean * scale
    zero = jnp.zeros((8, tile), jnp.float32)

    def body(k, sums, masked):
        at = pl.ds(pl.multiple_of(k * chunk, chunk), chunk)
        pre = hat[at, :]
        near = features[at, :] * jnp.bfloat16(0.5)
        half = pre * scale + offset + near.astype(jnp.float32)
        bent = jnp.tanh(half)
        up = 1.0 + bent
        value = half * up
        g = upstream[at, :].astype(jnp.float32) * (up + value * (1.0 - bent))
        if masked:
            used = row_ids(k * chunk, chunk, tile) < filled
            value = jnp.where(used, value, 0.0)
            g = jnp.where(used, g, 0.0)
        out[at, :] = value.astype(jnp.bfloat16)
        raw[at, :] = g
        grad[at, :] = g.astype(jnp.bfloat16)
        return (
            sums[0] + jnp.sum(g.reshape(chunk // 8, 8, tile), axis=0),
            sums[1] + jnp.sum((g * pre).reshape(chunk // 8, 8, tile), axis=0),
        )

    last = rows // chunk - 1
    sums = lax.fori_loop(0, last, lambda k, sums: body(k, sums, False), (zero, zero))
    sums = body(last, sums, True)
    first = column_sum(sums[0])
    second = inverse * (column_sum(sums[1]) - mean * first)
    put_rows(packed, stream, 0, 0.5 * first)
    put_rows(packed, stream, 2, 0.5 * second)
    tilt = scale * inverse * second / count
    level = scale * first / count - mean * tilt

    def centre(k, start, masked):
        at = pl.ds(start, chunk)
        value = raw[at, :] * scale - hat[at, :] * tilt - level
        if masked:
            value = jnp.where(row_ids(start, chunk, tile) < filled, value, 0.0)
        part[at, :] = value.astype(jnp.bfloat16)
        return k

    lax.fori_loop(0, last, lambda k, _: centre(0, pl.multiple_of(k * chunk, chunk), False), 0)
    centre(0, last * chunk, True)


def head_stage(ints, tables, tallies, gain, bias, low, expander, features, upstream, tiles=4):
    rows, width = low.shape
    wide = expander.shape[1]
    tile = wide // tiles
    col = lambda i: (0, i)
    fix = lambda i: (0, 0)
    return pl.pallas_call(
        head_kernel,
        grid=(tiles,),
        in_specs=[
            SM,
            *([pl.BlockSpec((4, tile), col)] * len(tables)),
            *([pl.BlockSpec((8, tile), fix)] * len(tables)),
            pl.BlockSpec((1, tile), col),
            pl.BlockSpec((1, tile), col),
            pl.BlockSpec((rows, width), fix),
            pl.BlockSpec((width, tile), col),
            pl.BlockSpec((rows, tile), col),
            pl.BlockSpec((rows, tile), col),
        ],
        out_specs=[
            pl.BlockSpec((rows, tile), col),
            pl.BlockSpec((rows, tile), col),
            pl.BlockSpec((rows, tile), col),
            pl.BlockSpec((4, tile), col),
            pl.BlockSpec((8, tile), col),
        ],
        out_shape=[
            struct((rows, wide), jnp.bfloat16),
            struct((rows, wide), jnp.bfloat16),
            struct((rows, wide), jnp.bfloat16),
            struct((4, wide)),
            struct((8, wide)),
        ],
        scratch_shapes=[
            pltpu.VMEM((rows, tile), jnp.float32),
            pltpu.VMEM((rows, tile), jnp.float32),
        ],
        compiler_params=params(42),
        cost_estimate=cost(2 * rows * width * wide, 32e6),
        name="head_stage",
    )(ints, *tables, *tallies, gain, bias, low, expander, features, upstream)


def cov_kernel(ints, low, centred, cov):
    filled = ints[1]
    values = low[...].astype(jnp.float32)
    centre = column_sum(values) / filled.astype(jnp.float32)
    centred[...] = fill(values - centre, filled).astype(jnp.bfloat16)
    cov[...] = dot_rows(centred[...], centred[...]).astype(jnp.bfloat16)


def cov_stage(ints, low):
    rows, width = low.shape
    return pl.pallas_call(
        cov_kernel,
        in_specs=[SM, VM],
        out_specs=[VM, VM],
        out_shape=[struct((rows, width), jnp.bfloat16), struct((width, width), jnp.bfloat16)],
        compiler_params=params(20),
        cost_estimate=cost(2 * rows * width * width, 5e6),
        name="cov_stage",
    )(ints, low)


def weight_kernel(low, part, out):
    out[...] = dot_rows(low[...], part[...])


def weight_stage(low, part, place, places):
    rows, width = low.shape
    tile = part.shape[1] // places
    return pl.pallas_call(
        weight_kernel,
        grid=(1,),
        in_specs=[
            pl.BlockSpec((rows, width), lambda i: (0, 0)),
            pl.BlockSpec((rows, tile), lambda i: (0, place)),
        ],
        out_specs=pl.BlockSpec((width, tile), lambda i: (0, 0)),
        out_shape=struct((width, tile)),
        compiler_params=params(28),
        cost_estimate=cost(2 * rows * width * tile, 8e6),
        name="weight_stage",
    )(low, part)


def back_kernel(part, expander, out):
    out[...] = dot_cols(part[...], expander[...])


def back_stage(part, expander, place, places):
    rows, wide = part.shape
    width = expander.shape[0]
    tile = rows // places
    return pl.pallas_call(
        back_kernel,
        grid=(1,),
        in_specs=[
            pl.BlockSpec((tile, wide), lambda i: (place, 0)),
            pl.BlockSpec((width, wide), lambda i: (0, 0)),
        ],
        out_specs=pl.BlockSpec((tile, width), lambda i: (0, 0)),
        out_shape=struct((tile, width)),
        compiler_params=params(28),
        cost_estimate=cost(2 * tile * width * wide, 8e6),
        name="back_stage",
    )(part, expander)


def split_pair(row):
    high = row.astype(jnp.bfloat16)
    return high, (row - high.astype(jnp.float32)).astype(jnp.bfloat16)


def turn_kernel(ints, *refs):
    tables, refs = refs[:-14], refs[-14:]
    local, local_moments, norm_last, expander, centred, upper, lower, pre, norm = refs[:9]
    grad, packed, scaled, shift, eight = refs[9:]
    filled, stream = ints[1], ints[2]
    rows, width = pre.shape
    count = filled.astype(jnp.float32)
    mean, inverse, gain = norm_last[0:1, :], norm_last[1:2, :], norm_last[2:3, :]
    number = norm_last[4:5, :]
    scale = gain * inverse
    first = sum_tables(tables, stream, 0)
    second = sum_tables(tables, stream, 2)
    off_first = scale * (first / number - pick(local, stream, 0) / count)
    off_second = inverse * scale * (second / number - pick(local, stream, 2) / count)
    line = off_first + (pick(local_moments, stream, 0) - mean) * off_second
    shift[...] = line
    scaled[...] = (expander[...].astype(jnp.float32) * off_second).astype(jnp.bfloat16)
    square = dot_cols(scaled[...], expander[...]).astype(jnp.bfloat16)
    high, rest = split_pair(line)
    eight[...] = jnp.zeros_like(eight)
    eight[0:1, :] = high.astype(jnp.float32)
    eight[1:2, :] = rest.astype(jnp.float32)
    flat = column_sum(dot_cols(eight[...].astype(jnp.bfloat16), expander[...]))
    half = rows // 2
    chunk = half // 2
    sums = []
    for k in range(rows // chunk):
        at = slice(k * chunk, (k + 1) * chunk)
        source = upper if k * chunk < half else lower
        back = source[k * chunk % half : k * chunk % half + chunk, :]
        normed = (pre[at, :] - norm[0:1, :]) * norm[1:2, :]
        slope = slope_of(normed * norm[2:3, :] + norm[3:4, :])
        value = (back - dot(centred[at, :], square) - flat) * slope
        value = fill(value, filled, k * chunk, rows)
        grad[at, :] = value
        sums.append((column_sum(value), column_sum(value * normed)))
    put_rows(packed, stream, 0, sum(first for first, _ in sums))
    put_rows(packed, stream, 2, sum(second for _, second in sums))


def turn_stage(
    ints, tables, local, local_moments, norm_last, expander, centred, upper, lower, pre, norm
):
    rows, width = pre.shape
    wide = expander.shape[1]
    return pl.pallas_call(
        turn_kernel,
        in_specs=[SM] + [VM] * (len(tables) + 9),
        out_specs=[VM] * 4,
        out_shape=[
            struct((rows, width)),
            struct((4, width)),
            struct((width, wide), jnp.bfloat16),
            struct((1, wide)),
        ],
        scratch_shapes=[pltpu.VMEM((8, wide), jnp.float32)],
        compiler_params=params(30),
        cost_estimate=cost(4 * width * width * wide, 12e6),
        name="turn_stage",
    )(
        ints, *tables, local, local_moments, norm_last, expander, centred, upper, lower, pre, norm
    )


def mend_kernel(ints, left_weight, right_weight, cov, scaled, shift, low, send, kept, left, right):
    sums = column_sum(low[...].astype(jnp.float32))
    sums_high, sums_rest = split_pair(sums)
    line_high, line_rest = split_pair(shift[...])
    left[...] = jnp.zeros_like(left)
    right[...] = jnp.zeros_like(right)
    for at, a, b in (
        (0, sums_high, line_high),
        (1, sums_rest, line_high),
        (2, sums_high, line_rest),
    ):
        left[at : at + 1, :] = a.astype(jnp.float32)
        right[at : at + 1, :] = b.astype(jnp.float32)
    lower = ints[3] == 0
    width = low.shape[1]

    def block(weight, at, place):
        outer = dot_rows(left[...].astype(jnp.bfloat16), right[:, place].astype(jnp.bfloat16))
        return weight[:, at] - dot(cov[...], scaled[:, place]) - outer

    for k in range(send.shape[0] // width):
        at = slice(k * lane, (k + 1) * lane)
        rows = slice(k * width, (k + 1) * width)
        shift_by = scaled.shape[1] // 2
        first = block(left_weight, at, at)
        second = block(right_weight, at, slice(shift_by + k * lane, shift_by + (k + 1) * lane))
        send[rows, :] = jnp.where(lower, second, first)
        kept[rows, :] = jnp.where(lower, first, second)


def mend_stage(ints, left_weight, right_weight, cov, scaled, shift, low):
    width, wide = scaled.shape
    return pl.pallas_call(
        mend_kernel,
        in_specs=[SM] + [VM] * 6,
        out_specs=[VM, VM],
        out_shape=[struct((width * wide // (2 * lane), lane))] * 2,
        scratch_shapes=[
            pltpu.VMEM((16, width), jnp.float32),
            pltpu.VMEM((16, wide), jnp.float32),
        ],
        compiler_params=params(32),
        cost_estimate=cost(2 * width * width * wide, 14e6),
        name="mend_stage",
    )(ints, left_weight, right_weight, cov, scaled, shift, low)


def norm_grad(grad, pre, norm, tables, stream):
    scale = norm[2:3, :] * norm[1:2, :]
    first = sum_tables(tables, stream, 0) / norm[4:5, :]
    second = sum_tables(tables, stream, 2) / norm[4:5, :]
    normed = (pre[...] - norm[0:1, :]) * norm[1:2, :]
    return scale * (grad[...] - first - normed * second)


def halves(product, core):
    half = product.shape[1] // 2
    left, right = product[:, :half], product[:, half:]
    return jnp.where(core == 0, right, left), jnp.where(core == 0, left, right)


def turned_kernel(low, turned):
    turned[...] = low[...].T


def turned_stage(low):
    rows, width = low.shape
    return pl.pallas_call(
        turned_kernel,
        in_specs=[VM],
        out_specs=VM,
        out_shape=struct((width, rows), low.dtype),
        compiler_params=params(16),
        cost_estimate=cost(0, 2e6),
        name="turned_stage",
    )(low)


def taps_kernel(ints, *refs):
    tables, refs = refs[:-11], refs[-11:]
    grad, pre, norm, turned, rounded, send, kept, weight, held, slots, sems = refs
    side, filled, stream = ints[0], ints[1], ints[2]
    rows, width = grad.shape
    value = fill(norm_grad(grad, pre, norm, tables, stream), filled)
    rounded[...] = value.astype(jnp.bfloat16)
    hold(held, value, rows)
    high, across = place(0, rows, side)
    copies = []
    for tap, (dr, dc) in enumerate(OFFSETS):
        piece = moved(held, pad - dr * side - dc, rows)
        if (dr, dc) != (0, 0):
            piece = jnp.where(spread(inside(high, across, side, -dr, -dc), width), piece, 0.0)
        product = dot(turned[...], piece.astype(jnp.bfloat16))
        if tap < shared:
            at = slice(tap * width, (tap + 1) * width)
            send[at, :], kept[at, :] = halves(product, ints[3])
            continue
        k = tap - shared
        if k >= 3:
            copies[k - 3].wait()
        slots[k % 3] = product
        at = pl.ds(k * width, width)
        copies.append(pltpu.make_async_copy(slots.at[k % 3], weight.at[at, :], sems.at[k % 3]))
        copies[k].start()
    for copy in copies[-3:]:
        copy.wait()


def taps_stage(ints, tables, grad, pre, norm, turned):
    rows, width = grad.shape
    return pl.pallas_call(
        taps_kernel,
        in_specs=[SM] + [VM] * (len(tables) + 4),
        out_specs=[VM, VM, VM, HBM],
        out_shape=[
            struct((rows, width), jnp.bfloat16),
            struct((shared * width, lane)),
            struct((shared * width, lane)),
            struct(((9 - shared) * width, width)),
        ],
        scratch_shapes=[
            pltpu.VMEM((rows + 3 * pad, width), jnp.float32),
            pltpu.VMEM((3, width, width), jnp.float32),
            pltpu.SemaphoreType.DMA((3,)),
        ],
        compiler_params=params(44),
        cost_estimate=cost(18 * rows * width * width, 18e6),
        name="taps_stage",
    )(ints, *tables, grad, pre, norm, turned)


def down_kernel(ints, rounded, pre, norm, spatial, grad, packed, held, weights, sems):
    side, filled, stream = ints[0], ints[1], ints[2]
    rows, width = pre.shape
    copies = stream_weights(spatial, weights, sems)
    hold(held, rounded[...].astype(jnp.float32), rows)
    high, across = place(0, rows, side)
    total = jnp.zeros((rows, width), jnp.float32)
    for tap, (dr, dc) in enumerate(OFFSETS):
        piece = moved(held, pad - dr * side - dc, rows)
        if (dr, dc) != (0, 0):
            piece = jnp.where(spread(inside(high, across, side, -dr, -dc), width), piece, 0.0)
        if tap % 3 == 0:
            copies[tap // 3].wait()
        total += dot_cols(piece.astype(jnp.bfloat16), weights[tap * width : (tap + 1) * width, :])
    grad[...] = total
    normed = (pre[...] - norm[0:1, :]) * norm[1:2, :]
    act = normed * norm[2:3, :] + norm[3:4, :]
    value = fill(grad[...] * slope_of(act), filled)
    grad[...] = value
    put_rows(packed, stream, 0, column_sum(value))
    put_rows(packed, stream, 2, column_sum(value * normed))


def down_stage(ints, rounded, spatial, pre, norm):
    rows, width = pre.shape
    return pl.pallas_call(
        down_kernel,
        in_specs=[SM] + [VM] * 3 + [HBM],
        out_specs=[VM, VM],
        out_shape=[struct((rows, width)), struct((4, width))],
        scratch_shapes=[
            pltpu.VMEM((rows + 3 * pad, width), jnp.float32),
            pltpu.VMEM(spatial.shape, jnp.bfloat16),
            pltpu.SemaphoreType.DMA((3,)),
        ],
        compiler_params=params(40),
        cost_estimate=cost(18 * rows * width * width, 14e6),
        name="down_stage",
    )(ints, rounded, pre, norm, spatial)


def root_kernel(ints, *refs):
    tables, refs = refs[:-7], refs[-7:]
    grad, pre, norm, features, low, send, kept = refs
    filled, stream, core = ints[1], ints[2], ints[3]

    @pl.when(pl.program_id(0) == 0)
    def _():
        value = fill(norm_grad(grad, pre, norm, tables, stream), filled)
        low[...] = value.astype(jnp.bfloat16)

    send[...], kept[...] = halves(dot_rows(features[...], low[...]), core)


def root_stage(ints, tables, grad, pre, norm, features, tiles=4):
    rows, width = grad.shape
    wide = features.shape[1]
    tile = wide // tiles
    fix = lambda i: (0, 0)
    return pl.pallas_call(
        root_kernel,
        grid=(tiles,),
        in_specs=[
            SM,
            *([pl.BlockSpec((4, width), fix)] * len(tables)),
            pl.BlockSpec((rows, width), fix),
            pl.BlockSpec((rows, width), fix),
            pl.BlockSpec((8, width), fix),
            pl.BlockSpec((rows, tile), lambda i: (0, i)),
        ],
        out_specs=[
            pl.BlockSpec((rows, width), fix),
            pl.BlockSpec((tile, width // 2), lambda i: (i, 0)),
            pl.BlockSpec((tile, width // 2), lambda i: (i, 0)),
        ],
        out_shape=[
            struct((rows, width), jnp.bfloat16),
            struct((wide, width // 2)),
            struct((wide, width // 2)),
        ],
        compiler_params=params(36),
        cost_estimate=cost(2 * rows * width * wide, 16e6),
        name="root_stage",
    )(ints, *tables, grad, pre, norm, features)


def input_kernel(low, reducer, grad, out):
    half = grad[...].astype(jnp.float32) * 0.5
    out[...] = (dot_cols(low[...], reducer[...]) + half).astype(jnp.bfloat16)


def input_stage(low, reducer, grad, tiles=4):
    rows, width = low.shape
    wide = reducer.shape[0]
    tile = wide // tiles
    return pl.pallas_call(
        input_kernel,
        grid=(tiles,),
        in_specs=[
            pl.BlockSpec((rows, width), lambda i: (0, 0)),
            pl.BlockSpec((tile, width), lambda i: (i, 0)),
            pl.BlockSpec((rows, tile), lambda i: (0, i)),
        ],
        out_specs=pl.BlockSpec((rows, tile), lambda i: (0, i)),
        out_shape=struct((rows, wide), jnp.bfloat16),
        compiler_params=params(30),
        cost_estimate=cost(2 * rows * width * wide, 22e6),
        name="input_stage",
    )(low, reducer, grad)


def halve_stage(ints, pairs, place):
    shapes = [struct(pair[0].shape) for pair in pairs]
    cuts = jax.eval_shape(lambda sums: [item[:2] for item in place(sums)], shapes)

    def kernel(ints, *refs):
        taken, given = refs[: 2 * len(pairs)], refs[2 * len(pairs) :]
        sums = [taken[2 * k][...] + taken[2 * k + 1][...] for k in range(len(pairs))]
        for k, (first, second, bit) in enumerate(place(sums)):
            lower = ints[3 + bit] == 0
            given[2 * k][...] = jnp.where(lower, second, first)
            given[2 * k + 1][...] = jnp.where(lower, first, second)

    out = [struct(half.shape) for item in cuts for half in item]
    return pl.pallas_call(
        kernel,
        in_specs=[SM] + [VM] * (2 * len(pairs)),
        out_specs=[VM] * len(out),
        out_shape=out,
        compiler_params=params(24),
        cost_estimate=cost(0, 4 * sum(half.size for half in out)),
        name="halve_stage",
    )(ints, *[value for pair in pairs for value in pair])


def order_stage(ints, pairs, bits, together):
    rows = [pair[0].shape[0] for pair in pairs]
    width = pairs[0][0].shape[1]

    def kernel(ints, *refs):
        taken, given = refs[: 2 * len(pairs)], refs[2 * len(pairs) :]
        start = 0
        for k, bit in enumerate(bits):
            own, other = taken[2 * k][...], taken[2 * k + 1][...]
            lower = ints[3 + bit] == 0
            out = given[0 if together else k]
            out[start : start + rows[k], :] = jnp.where(lower, own, other)
            out[start + rows[k] : start + 2 * rows[k], :] = jnp.where(lower, other, own)
            start = start + 2 * rows[k] if together else 0

    shapes = [2 * sum(rows)] if together else [2 * count for count in rows]
    return pl.pallas_call(
        kernel,
        in_specs=[SM] + [VM] * (2 * len(pairs)),
        out_specs=[VM] * len(shapes),
        out_shape=[struct((count, width)) for count in shapes],
        compiler_params=params(24),
        cost_estimate=cost(0, 16 * sum(rows) * width),
        name="order_stage",
    )(ints, *[value for pair in pairs for value in pair])


def settle_stage(ints, upper, lower, height, spatial_held):
    width = upper[0].shape[1]
    first = height // 8
    second = upper[0].shape[0] // 4 - first

    def kernel(ints, own, other, own_too, other_too, held, out, out_too):
        mine = jnp.where(pl.program_id(0) < 4, own[...], own_too[...])
        others = jnp.where(pl.program_id(0) < 4, other[...], other_too[...])
        left = jnp.where(ints[3] == 0, mine, others)
        right = jnp.where(ints[3] == 0, others, mine)
        out[:, :width] = left[:first]
        out[:, width:] = right[:first]
        out_too[:, :width] = left[first:]
        out_too[:, width:] = right[first:]

    early = pl.BlockSpec((first + second, width), lambda i: (jnp.minimum(i, 3), 0))
    late = pl.BlockSpec((first + second, width), lambda i: (jnp.maximum(i - 4, 0), 0))
    return pl.pallas_call(
        kernel,
        grid=(8,),
        in_specs=[SM, early, early, late, late, ANY],
        out_specs=[
            pl.BlockSpec((first, 2 * width), lambda i: (i, 0)),
            pl.BlockSpec((second, 2 * width), lambda i: (i, 0)),
        ],
        out_shape=[struct((height, 2 * width)), struct(spatial_held.shape)],
        input_output_aliases={5: 1},
        compiler_params=params(32),
        cost_estimate=cost(0, 32 * upper[0].size),
        name="settle_stage",
    )(ints, *upper, *lower, spatial_held)


def join_blocks(ints, upper, lower, height):
    rows, width = upper[0].shape
    count = rows // height

    def kernel(ints, own, other, own_too, other_too, out):
        step = pl.program_id(0)
        mine = (step // (2 * count)) == ints[3]
        second = (step % (2 * count)) >= count
        for is_mine in (True, False):
            for is_second in (True, False):

                @pl.when((mine == is_mine) & (second == is_second))
                def _():
                    source = (own_too if is_second else own) if is_mine else (
                        other_too if is_second else other
                    )
                    out[...] = source[...]

    spec = pl.BlockSpec((height, width), lambda i: (i % count, 0))
    return pl.pallas_call(
        kernel,
        grid=(4 * count,),
        in_specs=[SM, spec, spec, spec, spec],
        out_specs=pl.BlockSpec((height, width), lambda i: (0, i)),
        out_shape=struct((height, 4 * count * width)),
        compiler_params=params(24),
        cost_estimate=cost(0, 16 * 2 * upper[0].size),
        name="join_blocks",
    )(ints, *upper, *lower)


def lower_kernel(lower, out, held, sems):
    tile = held.shape[1]
    count = held.shape[0]
    first = out.shape[0] - lower.shape[0]
    comes, goes = [], []
    for k in range(count):
        start = k * tile
        comes.append(
            pltpu.make_async_copy(lower.at[pl.ds(start, tile), :], held.at[k], sems.at[0, k])
        )
        goes.append(
            pltpu.make_async_copy(held.at[k], out.at[pl.ds(first + start, tile), :], sems.at[1, k])
        )
        comes[k].start()
    for come, go in zip(comes, goes):
        come.wait()
        go.start()
    for go in goes:
        go.wait()


def lower_stage(lower, rows, tile=512):
    width = lower.shape[1]
    count = lower.shape[0] // tile
    return pl.pallas_call(
        lower_kernel,
        in_specs=[ANY],
        out_specs=ANY,
        out_shape=struct((rows, width)),
        scratch_shapes=[
            pltpu.VMEM((count, tile, width), jnp.float32),
            pltpu.SemaphoreType.DMA((2, count)),
        ],
        compiler_params=params(20),
        cost_estimate=cost(0, 8 * rows * width),
        name="lower_stage",
    )(lower)


class Wide:
    def __init__(self, devices):
        self.devices = devices
        self.bits = [1 << k for k in range(devices.bit_length() - 1)]

    def swap(self, value, bit):
        pairs = [(i, i ^ bit) for i in range(self.devices)]
        return lax.ppermute(value, "wide", pairs)

    def place(self, bit):
        return ((lax.axis_index("wide") & bit) != 0).astype(jnp.int32)

    def groups(self, wide_steps):
        rest = self.bits[1:]
        if not wide_steps:
            return [[bit] for bit in self.bits]
        steps = [rest[k : k + 2] for k in range(0, len(rest), 2)]
        return [[self.bits[0]]] + [
            step if len(step) == 1 else [step[0], step[1], step[0] + step[1]] for step in steps
        ]

    def exchange(self, packed, step, job):
        if job is None:
            return [self.swap(packed, bit) for bit in step], None
        function, arrays = job
        packed, arrays = lax.optimization_barrier((packed, arrays()))
        return lax.optimization_barrier(
            ([self.swap(packed, bit) for bit in step], function(*arrays))
        )

    def merge(self, packed, tallies, jobs={}):
        results = {}
        steps = self.groups(True)

        def join(left, right):
            (mean, square, count, tail), (other_mean, other_square, other_count, _) = left, right
            mean, square, count = join_moments(
                (mean, square, count), (other_mean, other_square, other_count)
            )
            return mean, square, count, tail

        for at, step in enumerate(steps):
            others, results[at] = self.exchange(packed, step, jobs.get(at))
            tables = [packed] + others
            if at == len(tallies):
                tallies.append(tables)
            if at == len(steps) - 1:
                return tables, results
            full = packed.shape[0] == 8
            mean, square, count, tail = pair_up(
                [
                    (table[0:2], table[2:4], tally[4:6, : None if full else 1], tally[6:8])
                    for table, tally in zip(tables, tallies[at])
                ],
                join,
            )
            packed = jnp.concatenate([mean, square] + ([count, tail] if full else []), axis=0)

    def total(self, packed, jobs={}, wide_steps=True):
        results = {}
        steps = self.groups(wide_steps)
        for at, step in enumerate(steps):
            others, results[at] = self.exchange(packed, step, jobs.get(at))
            tables = [packed] + others
            if at == len(steps) - 1:
                return tables, results
            packed = pair_up(tables, lambda a, b: a + b)

    def first_round(self, ints, pairs):
        def quarters(sums):
            pieces = []
            for k in range(4):
                parts = []
                for value in sums:
                    rows = value.shape[0] // 4
                    step = rows // 2
                    parts.append([value[k * rows : k * rows + step], value[k * rows + step : (k + 1) * rows]])
                pieces.append(
                    jnp.concatenate([part[h] for h in (0, 1) for part in parts], axis=0)
                    if len(sums) > 1
                    else sums[0][k * rows : (k + 1) * rows]
                )
            return [(pieces[0], pieces[1], 1), (pieces[2], pieces[3], 2)]

        send, keep, send_too, keep_too = halve_stage(ints, pairs, quarters)
        return [keep, keep_too], [(send, 1), (send_too, 2)]

    def second_round(self, ints, keeps, gets):
        pairs = [(keep[part], get[part]) for part in (0, 1) for keep, get in zip(keeps, gets)]

        def place(sums):
            cuts = []
            for at, bit in ((0, 2), (len(keeps), 1)):
                part = sums[at : at + len(keeps)]
                halves = [
                    [value[: value.shape[0] // 2] for value in part],
                    [value[value.shape[0] // 2 :] for value in part],
                ]
                halves = [
                    half[0] if len(half) == 1 else jnp.concatenate(half, axis=0) for half in halves
                ]
                cuts.append((*halves, bit))
            return cuts

        send, keep, send_too, keep_too = halve_stage(ints, pairs, place)
        return [keep, keep_too], [(send, 2), (send_too, 1)]

    def rounds(self, ints, kept, wanted):
        rest = list(range(3, len(self.bits)))
        gets = yield wanted
        send, keep = halve_stage(
            ints, list(zip(kept, gets)), lambda sums: [(sums[0], sums[1], rest[0])]
        )
        (get,) = yield [(send, rest[0])]
        for bit in rest[1:]:

            def place(sums):
                rows = sums[0].shape[0] // 2
                return [(sums[0][:rows], sums[0][rows:], bit)]

            send, keep = halve_stage(ints, [(keep, get)], place)
            (get,) = yield [(send, bit)]
        value = keep + get
        for bit in rest[:0:-1]:
            (get,) = yield [(value, bit)]
            (value,) = order_stage(ints, [(value, get)], [bit], True)
        (get,) = yield [(value, rest[0])]
        lower = ints[3 + rest[0]] == 0
        value, value_too = jnp.where(lower, value, get), jnp.where(lower, get, value)
        get, get_too = yield [(value, 2), (value_too, 1)]
        value, value_too = order_stage(ints, [(value, get), (value_too, get_too)], [2, 1], False)
        return value, value_too

    def last_rounds(self, ints, value, value_too):
        get, get_too = yield [(value, 1), (value_too, 2)]
        value, value_too = order_stage(ints, [(value, get), (value_too, get_too)], [1, 2], False)
        get, get_too = yield [(value, 0), (value_too, 0)]
        return (value, get), (value_too, get_too)

    def send(self, wanted):
        return [self.swap(value, self.bits[bit]) for value, bit in wanted]


class Bulk:
    def __init__(self, wide, steps):
        self.wide = wide
        self.steps = steps
        self.result = None
        self.launch(next(self.steps))

    def launch(self, wanted):
        self.sends = [value for value, _ in wanted]
        self.flight = self.wide.send(wanted)

    def land(self, values):
        if self.result is not None:
            return values
        values, self.flight = lax.optimization_barrier((values, self.flight))
        self.advance()
        return values

    def advance(self):
        try:
            self.launch(self.steps.send(self.flight))
        except StopIteration as stop:
            self.result = stop.value
            self.sends = list(stop.value)


def on_device(
    wide,
    features,
    group_ids,
    reducer,
    spatial,
    expander,
    gain_first,
    bias_first,
    gain_middle,
    bias_middle,
    gain_last,
    bias_last,
    upstream,
):
    rows = features.shape[0]
    group = group_ids[0]
    side = jnp.where(group == 3, 2, 5 + group)
    area = side * side
    ints = jnp.stack(
        [side, (rows // area) * area, (group == 3).astype(jnp.int32)]
        + [wide.place(bit) for bit in wide.bits]
    ).astype(jnp.int32)
    line = lambda values: values[None, :]
    tallies = []
    plus = lambda tables: pair_up(tables, lambda a, b: a + b)

    pre_first, packed = first_stage(ints, features, reducer)
    tables, _ = wide.merge(packed, tallies)
    tally = tables
    low_first, pre_middle, packed, norm_first = middle_stage(
        ints, tables, line(gain_first), line(bias_first), pre_first, spatial
    )
    tables, _ = wide.merge(packed, tallies)
    low_middle, moments_last, norm_middle = last_stage(
        ints, tables, tally, line(gain_middle), line(bias_middle), pre_middle, expander
    )
    tables, done = wide.merge(
        moments_last, tallies, {1: (lambda low: cov_stage(ints, low), lambda: (low_middle,))}
    )
    centred, cov = done[1]
    block_out, grad_summed, part, local, norm_last = head_stage(
        ints, tables, tally, line(gain_last), line(bias_last), low_middle, expander, features,
        upstream,
    )
    feed = lambda: (part,)
    tables, done = wide.total(
        local,
        {
            1: (lambda part: back_stage(part, expander, 0, 2), feed),
            2: (lambda part: back_stage(part, expander, 1, 2), feed),
            3: (lambda part: weight_stage(low_middle, part, 0, 2), feed),
            4: (lambda part: weight_stage(low_middle, part, 1, 2), feed),
        },
        False,
    )
    sums_last = plus(tables)
    grad_middle, packed, scaled, shift = turn_stage(
        ints, tables, local, moments_last, norm_last, expander, centred, done[1], done[2],
        pre_middle, norm_middle,
    )
    store = {}

    def mend(*arrays):
        store["send"], store["kept"] = mend_stage(ints, *arrays)
        return store["kept"]

    def turned(low, send):
        store["other"] = wide.swap(send, wide.bits[0])
        return turned_stage(low)

    def leave(kept, other):
        kept, wanted = wide.first_round(ints, [(kept, other)])
        store["flight"] = (kept, wide.send(wanted))
        return [value for value, _ in wanted]

    tables, done = wide.total(
        packed,
        {
            1: (mend, lambda: (done[3], done[4], cov, scaled, shift, low_middle)),
            2: (turned, lambda: (low_first, store["send"])),
            3: (leave, lambda: (store["kept"], store["other"])),
        },
        False,
    )
    sums_early = [plus(tables), sums_last]
    rounded, send, kept, spatial_part = taps_stage(
        ints, tables, grad_middle, pre_middle, norm_middle, done[2]
    )
    (rounded, spatial_part), flight = lax.optimization_barrier(
        ((rounded, spatial_part), store["flight"])
    )
    spatial_rest = lax.psum(spatial_part, "wide")

    def finish(rounded, flight, kept_too, send_too):
        other_too = wide.swap(send_too, wide.bits[0])
        kept, wanted = wide.second_round(ints, [flight[0]], [flight[1]])
        rounded, _ = lax.optimization_barrier((rounded, wanted[0][0]))
        bulk_last = Bulk(wide, wide.rounds(ints, kept, wanted))
        grad_first, packed = down_stage(ints, rounded, spatial, pre_first, norm_first)
        packed, bulk_last.flight, other_too = lax.optimization_barrier(
            (packed, bulk_last.flight, other_too)
        )
        def third(*flight):
            store["wanted"] = bulk_last.steps.send(flight)
            return [value for value, _ in store["wanted"]]

        tables, done = wide.total(packed, {1: (third, lambda: bulk_last.flight)})
        tables, sends = lax.optimization_barrier((tables, done[1]))
        bulk_last.launch([(value, bit) for value, (_, bit) in zip(sends, store["wanted"])])
        sums = [plus(tables), *sums_early]
        sums = [(table[2] + table[3], table[0] + table[1]) for table in sums]
        low_grad, send, kept = root_stage(
            ints, tables, grad_first, pre_first, norm_first, features
        )
        other = wide.swap(send, wide.bits[0])
        kept, wanted = wide.first_round(ints, [(kept, other), (kept_too, other_too)])
        low_grad, _ = lax.optimization_barrier((low_grad, wanted[0][0]))
        gets = wide.send(wanted)
        features_grad = input_stage(low_grad, reducer, grad_summed)
        bulk_last.flight, features_grad = lax.optimization_barrier(
            (bulk_last.flight, features_grad)
        )
        bulk_last.advance()
        features_grad, _ = lax.optimization_barrier((features_grad, bulk_last.sends))
        gets, features_grad, sums = lax.optimization_barrier((gets, features_grad, sums))
        kept, wanted = wide.second_round(ints, [kept], [gets])
        bulk_first = Bulk(wide, wide.rounds(ints, kept, wanted))
        finished = False
        while bulk_first.result is None:
            features_grad, _ = lax.optimization_barrier((features_grad, bulk_first.sends))
            if bulk_last.result is None:
                bulk_last.flight, features_grad = lax.optimization_barrier(
                    (bulk_last.flight, features_grad)
                )
                bulk_last.advance()
                if bulk_last.result is not None and not finished:
                    finished = True
                    bulk_last = Bulk(wide, wide.last_rounds(ints, *bulk_last.result))
                features_grad, _ = lax.optimization_barrier((features_grad, bulk_last.sends))
            features_grad = bulk_first.land(features_grad)
        while bulk_last.result is None:
            features_grad = bulk_last.land(features_grad)
        expander_grad = join_blocks(ints, *bulk_last.result, expander.shape[0])
        return features_grad, expander_grad, sums, bulk_first.result

    def nothing(rounded, flight, kept_too, send_too):
        width = reducer.shape[1]
        part = reducer.shape[0] + shared * width
        return (
            jnp.zeros(features.shape, jnp.bfloat16),
            jnp.zeros(expander.shape, jnp.float32),
            [(jnp.zeros((count,)), jnp.zeros((count,))) for count in (width, width, features.shape[1])],
            (jnp.zeros((part // 4, lane)), jnp.zeros((part // 4, lane))),
        )

    features_grad, expander_grad, sums, values = lax.cond(
        group >= 0, finish, nothing, rounded, flight, kept, send
    )
    bulk_first = Bulk(wide, wide.last_rounds(ints, *values))
    bulk_first.advance()
    spatial_rest, _ = lax.optimization_barrier((spatial_rest, bulk_first.sends))
    spatial_grad = lower_stage(spatial_rest, spatial.shape[0])
    bulk_first.flight, spatial_grad = lax.optimization_barrier(
        (bulk_first.flight, spatial_grad)
    )
    reducer_grad, spatial_grad = settle_stage(
        ints, *zip(bulk_first.sends, bulk_first.flight), reducer.shape[0], spatial_grad
    )
    return (
        block_out,
        features_grad,
        reducer_grad,
        spatial_grad,
        expander_grad,
        *[row for pair in sums for row in pair],
    )


def solution(mesh):
    wide = Wide(mesh.shape["wide"])
    in_specs = (
        P("wide", None),
        P("wide"),
        P(),
        P(),
        P(),
        P(),
        P(),
        P(),
        P(),
        P(),
        P(),
        P("wide", None),
    )
    out_specs = (P("wide", None), P("wide", None), P(), P(), P(), P(), P(), P(), P(), P(), P())

    def body(*arrays):
        return on_device(wide, *arrays)

    return jax.shard_map(body, mesh=mesh, in_specs=in_specs, out_specs=out_specs, check_vma=False)
```
